32 devices in a mesh: groups: 2 (over x), bond: 8 (over z, y), term: 2 (over core).
Axes of the slice: x: 2, y: 2, z: 4, core: 2. Of those that a mesh axis runs over, the one named last changes fastest.
Arguments:
- psi_blocks: float32 [768, 128, 128], P(('groups', 'bond')), parts along dimension 0, may hold values from -6 to 6
- left_env: float32 [12, 48, 128, 128], P('term', ('groups', 'bond')), parts along dimension 1, may hold values from -0.0140625 to 4
- right_env: float32 [12, 48, 128, 128], P('term', ('groups', 'bond')), parts along dimension 1, may hold values from -0.001171875 to 0.33333333
- owner_route: int32 [768, 1], P(('groups', 'bond')), parts along dimension 0, may hold values from 0 to 7; in each aligned block of 48 rows (0 to 47, 48 to 95, ...) at most 9 rows name the same one
- local_sector: int32 [768], P(('groups', 'bond')), parts along dimension 0, may hold values from 0 to 2
Outputs:
- residual: float32 [768, 128, 128], P(('groups', 'bond')), parts along dimension 0
- theta: float32 [2], P('groups'), parts along dimension 0
The draws below stay inside these ranges and needn't reach their ends.
There are 2 independent parts, one for each index of `groups`. The reference program is written for one: setup_inputs(seed, part) draws one part's arguments, and reference() takes and returns one part's arrays. A program takes and returns all parts, laid end to end along the dimension named above; each array names one. Nothing has to cross between parts.
Inputs may be any that keep to these rules, and one draw needn't show every extreme that they name: `owner_route`: among the 48 blocks of one device, no owner index is named more than 9 times, a bound that some block reaches.
All inputs are finite; a program needn't handle non-finite values.
Results may differ from the reference program's by a relative error of at most 0.0003.
Values sent between devices are 32-bit elements; how exact they have to be, the bound alone decides.
A program may use at most 256 MiB of HBM per device.

```python
import math
import jax
import jax.numpy as jnp
import numpy as np
from jax import lax

MS = 128
MB = 12
PH = 16
SEC_DEV = 3
BLK_DEV = 48
SECTORS = 24
BLOCKS = 384
CAP = 9
N_BOND = 8


def general_env(key, top):
    first, second = jax.random.split(key)
    raw = jax.random.uniform(first, (MB, SECTORS, MS, MS), jnp.float32, -1.0, 1.0)
    off_part = raw * (1.8 / MS)
    diag_part = jax.random.uniform(second, (MB, SECTORS, MS, 1), jnp.float32, 1.9, top)
    marker = jnp.arange(MS)[:, None] == jnp.arange(MS)[None, :]
    return jnp.where(marker, diag_part, off_part)


def draw_left_env(key, part):
    key = jax.random.fold_in(key, 11)
    top = 2.9
    return general_env(key, top)


def draw_right_env(key, part):
    key = jax.random.fold_in(key, 12)
    top = 2.9
    return general_env(key, top) / MB


def set_ends(entries, own_key, low, high):
    place = [jax.random.randint(jax.random.fold_in(own_key, axis), (), 0, length) for axis, length in enumerate(entries.shape)]
    longest = entries.shape.index(max(entries.shape))
    neighbour = place[:longest] + [(place[longest] + 1) % entries.shape[longest]] + place[longest + 1:]
    return entries.at[tuple(place)].set(low).at[tuple(neighbour)].set(high)


def shard_levels(rng, shape, shards, smallest, high):
    factor_of = 1.0
    for dim, blocks in shards:
        draws = jax.random.uniform(jax.random.fold_in(jax.random.fold_in(rng, 6), dim), (blocks,), jnp.float32, smallest / len(shards), high / len(shards))
        factor_of = factor_of * jnp.repeat(jnp.exp(draws), shape[dim] // blocks).reshape((-1,) + (1,) * (len(shape) - 1 - dim))
    return factor_of


def assign_block(key, own, number, rows, number_of, top, reach, skew):
    ranking = jax.random.permutation(key, number_of)
    heavy_load, common = load_shares(number_of, rows * top, reach, skew, True), load_shares(number_of, rows * top, reach, skew, False)
    places = jnp.arange(number_of)

    def named(sizes, turn):
        used = int((sizes > 0).sum())
        fixed = max(1, used // 4)
        moved = fixed + (places - fixed + turn * (used - fixed)) % max(1, number_of - fixed)
        return jnp.zeros((number_of,), jnp.int32).at[ranking[jnp.where(places < fixed, places, moved)]].set(jnp.asarray(sizes, jnp.int32))

    sizes = jnp.where(number % 4 == 0, named(heavy_load, number // 4), named(common, number - number // 4 - 1))
    mixed = jax.random.permutation(jax.random.fold_in(own, 3), number_of)
    donor, receiver = mixed[0:number_of // 2 * 2:2], mixed[1:number_of // 2 * 2:2]
    margin = jnp.minimum(sizes[donor] - 1, reach - sizes[receiver]) // 2
    margin = jnp.where((donor == ranking[0]) | (receiver == ranking[0]) | (sizes[receiver] == 0), 0, jnp.maximum(margin, 0))
    moved = jax.random.randint(jax.random.fold_in(own, 4), (number_of // 2,), 0, 1 << 20) % (margin + 1)
    sizes = sizes.at[donor].add(-moved).at[receiver].add(moved)
    members = jnp.searchsorted(jnp.cumsum(sizes), jnp.arange(rows * top), side="right").astype(jnp.int32)
    table = members.reshape(top, rows).T
    table = table[jax.random.permutation(jax.random.fold_in(own, 1), rows)]
    turn = jax.random.randint(jax.random.fold_in(own, 2), (rows, 1), 0, top)
    return jnp.take_along_axis(table, (jnp.arange(top)[None, :] + turn) % top, axis=1)


def load_shares(amount, total, limit, slope, full):
    portions = [(1 << 20) // math.isqrt(standing ** slope) + 1 for standing in range(1, amount + 1)]
    largest = limit if full else min(limit, max(-(-total // amount), total * portions[0] // sum(portions)))
    least = 1 if total - largest >= amount - 1 else 0
    counts, spare = [largest] + [least] * (amount - 1), total - largest - least * (amount - 1)
    while spare > 0:
        free = [i for i in range(1, amount) if counts[i] < largest] or [i for i in range(1, amount) if counts[i] < limit]
        whole, remaining = sum([portions[i] for i in free]), spare
        for i in free:
            more = min(limit - counts[i], max(1, remaining * portions[i] // whole), spare)
            counts[i] = counts[i] + more
            spare = spare - more
    return np.array(counts)


def gaussian(own_key, shape, deviation, bound, cuts=(), held_as=jnp.bfloat16):
    gain = shard_levels(own_key, shape, cuts, -0.22, 0.18) if cuts else 1.0
    drawn = jax.random.normal(own_key, shape, jnp.float32) * deviation * gain
    return jnp.minimum(jnp.maximum(drawn, -bound), bound).astype(held_as)


def setup_inputs(seed: int = 0, part: int = 0) -> dict:
    arg_keys = jax.random.split(jax.random.key(seed), 6)
    part_keys = jax.random.split(jax.random.fold_in(arg_keys[5], part), 6)
    psi_blocks = gaussian(part_keys[0], (BLOCKS, MS, MS), 1.0, 6.0, ((0, 8),), jnp.float32)
    left_env = draw_left_env(jax.random.fold_in(jax.random.fold_in(arg_keys[5], part), 71), part)
    right_env = draw_right_env(jax.random.fold_in(jax.random.fold_in(arg_keys[5], part), 71), part)
    owner_route_keys = jax.random.split(jax.random.fold_in(part_keys[3], 1), BLOCKS // BLK_DEV)
    owner_route_turns = jax.random.permutation(jax.random.fold_in(part_keys[3], 3), BLOCKS // BLK_DEV)
    owner_route = jax.vmap(lambda own, number: assign_block(jax.random.fold_in(part_keys[3], 2), own, number, BLK_DEV, N_BOND, 1, CAP, 2))(owner_route_keys, owner_route_turns).reshape((BLOCKS, 1))
    local_sector = set_ends(jax.random.randint(part_keys[4], (BLOCKS,), 0, SEC_DEV), jax.random.fold_in(part_keys[4], 1), 0, SEC_DEV - 1).astype(jnp.int32)
    return dict(psi_blocks=psi_blocks, left_env=left_env, right_env=right_env, owner_route=owner_route, local_sector=local_sector)


def reference(psi_blocks, left_env, right_env, owner_route, local_sector):
    right_sector = (owner_route[:, 0] * SEC_DEV + local_sector).astype(jnp.int32)
    left_sector = (jnp.arange(BLOCKS, dtype=jnp.int32) // PH).astype(jnp.int32)

    def one_block(items):
        block, left_index, right_index = items
        lefts = jnp.take(left_env, left_index, axis=1)
        rights = jnp.take(right_env, right_index, axis=1)
        inner = jnp.einsum("aij,jk->aik", lefts, block, precision=lax.Precision.HIGHEST)
        return jnp.einsum("aik,akl->il", inner, rights, precision=lax.Precision.HIGHEST)

    hpsi = lax.map(one_block, (psi_blocks, left_sector, right_sector))
    correlation = jnp.sum(psi_blocks * hpsi)
    norm_sum = jnp.sum(psi_blocks * psi_blocks)
    theta = correlation / norm_sum
    residual = hpsi - theta * psi_blocks
    return residual, jnp.reshape(theta, (1,))
```

```python
import functools

import jax
import jax.numpy as jnp
from jax import lax
from jax.experimental import pallas as pl
from jax.experimental.pallas import tpu as pltpu
from jax.sharding import PartitionSpec as P

MESH = pl.DeviceIdType.MESH
UP, DOWN, ACROSS = 0, 1, 2
NZ, NY = 4, 2
AHEAD = 2
F32, BF16 = jnp.float32, jnp.bfloat16


def split(x):
    hi = x.astype(BF16)
    lo = (x - hi.astype(F32)).astype(BF16)
    return hi, lo


def pair_rhs(x):
    hi, lo = split(x)
    row = jnp.concatenate([hi, lo], axis=1)
    return jnp.concatenate([row, row], axis=0)


def fold(o):
    n = o.shape[1] // 2
    return o[:, :n] + o[:, n:]


def rows_sum(x):
    r, c = x.shape
    return jnp.sum(x.reshape(r // 8, 8, c), axis=0)


def kernel(terms, sectors, phys, idx_ref, psi_hbm, left_hbm, right_hbm,
           part_hbm, other_hbm, theta_ref, *scratch):
    gathered = scratch[:terms]
    (psi_v, left_v, lefts, prods, acc, dots,
     recv, send, psi_sem, left_sem, own_sem, xsend, xrecv, out_sem, dsend, drecv) = scratch[terms:]
    bond_count = NZ * NY
    blocks = sectors * phys
    states = psi_v.shape[1]
    me = lax.axis_index("bond")
    core = lax.axis_index("term")
    z, y = me // NY, me % NY
    last = terms - 1

    def rows(src):
        return pl.ds(src * sectors, sectors)

    left_copy = pltpu.make_async_copy(left_hbm, left_v, left_sem)
    left_copy.start()
    psi_copies = []
    for s in range(sectors):
        c = pltpu.make_async_copy(psi_hbm.at[pl.ds(s * phys, phys)], psi_v.at[pl.ds(s * phys, phys)], psi_sem.at[s])
        c.start()
        psi_copies.append(c)
    own_copies = []
    for a in range(terms):
        c = pltpu.make_async_copy(right_hbm.at[a], gathered[a].at[rows(me)], own_sem.at[a])
        c.start()
        own_copies.append(c)

    barrier = pltpu.get_barrier_semaphore()
    peers = []
    for k in range(1, 2 * bond_count):
        flat = lax.rem(me * 2 + core + k, 2 * bond_count)
        peers.append((flat // 2, flat % 2))
    for pb, pt in peers:
        pl.semaphore_signal(barrier, inc=1, device_id={"bond": pb, "term": pt}, device_id_type=MESH)
    pl.semaphore_wait(barrier, len(peers))

    def chunk(a, src, way, own=False):
        if way == UP:
            to = me + NY
        elif way == DOWN:
            to = me - NY
        else:
            to = z * NY + (1 - y)
        here = right_hbm.at[a] if own else gathered[a].at[rows(src)]
        return pltpu.make_async_remote_copy(
            src_ref=here, dst_ref=gathered[a].at[rows(src)],
            send_sem=send.at[a, src, way], recv_sem=recv.at[a, src],
            device_id={"bond": to}, device_id_type=MESH)

    sent = []

    def go(cond, a, src, way, own=False):
        def start():
            chunk(a, src, way, own).start()

        if cond is None:
            start()
        else:
            pl.when(cond)(start)
        sent.append((cond, a, src, way, own))

    def arrived(a, src):
        chunk(a, src, ACROSS).wait_recv()

    partner = z * NY + (1 - y)

    def send_own(a):
        if a < last:
            go(z < NZ - 1, a, me, UP, True)
            go(z > 0, a, me, DOWN, True)
            go(None, a, me, ACROSS, True)
        else:
            go(z < NZ - 1, a, me, UP, True)
            go(z > 0, a, me, DOWN, True)
            arrived(a, partner)
            go(z < NZ - 1, a, partner, UP)
            go(z > 0, a, partner, DOWN)

    def prepare_left():
        left_copy.wait()
        for s in range(sectors):
            for a in range(terms):
                hi, lo = split(left_v[a, s])
                lefts[s, a * states:(a + 1) * states, :] = jnp.concatenate([hi, lo], axis=1)

    def left_piece(s, lo, count):
        def body(i, norm):
            b = s * phys + lo + i
            x = psi_v[b]
            t = fold(jnp.dot(lefts[s], pair_rhs(x), preferred_element_type=F32))
            hi, low = split(t)
            both = jnp.concatenate([hi, low], axis=1)
            for a in range(terms):
                prods[a, b] = both[a * states:(a + 1) * states]
            return norm + rows_sum(x * x)

        norm = lax.fori_loop(0, count, body, jnp.zeros((8, states), F32))
        dots[me * 2 + core, 8:16, :] += norm

    def right_piece(a, first, count):
        def body(i, dot):
            b = first + i
            w = pair_rhs(gathered[a][idx_ref[b]])
            v = fold(jnp.dot(prods[a, b], w, preferred_element_type=F32))
            if a > 0:
                v = v + acc[b]
            acc[b] = v
            if a == last:
                dot = dot + rows_sum(v * psi_v[b])
            return dot

        dot = lax.fori_loop(0, count, body, jnp.zeros((8, states), F32))
        if a == last:
            dots[me * 2 + core, 0:8, :] += dot

    def across_done(a):
        own_copies[a].wait()
        for zz in range(NZ):
            arrived(a, zz * NY + (1 - y))

    exchange = []

    def exchange_piece(k, first, count):
        c = pltpu.make_async_remote_copy(
            src_ref=acc.at[pl.ds(first, count)], dst_ref=other_hbm.at[pl.ds(first, count)],
            send_sem=xsend.at[k], recv_sem=xrecv.at[k],
            device_id={"term": 1 - core}, device_id_type=MESH)
        c.start()
        d = pltpu.make_async_copy(acc.at[pl.ds(first, count)], part_hbm.at[pl.ds(first, count)], out_sem.at[k])
        d.start()
        exchange.append((c, d))

    half = phys // 4
    left_work = []
    for s in range(sectors):
        for q in range(4):
            def piece(s=s, q=q):
                if q == 0:
                    psi_copies[s].wait()
                left_piece(s, q * half, half)
            left_work.append(piece)
    eighth = blocks // 6

    def right_work(a):
        out = []
        for q in range(6):
            def piece(a=a, q=q):
                if q == 0:
                    across_done(a)
                right_piece(a, q * eighth, eighth)
            out.append(piece)
        return out

    slots = {(a, k): [] for a in range(terms) for k in range(6)}
    for i, w in enumerate(left_work):
        slots[(i // 6, i % 6)].append(w)
    for a in range(terms - 2):
        for i, w in enumerate(right_work(a)):
            slots[(a + 2, i)].append(w)

    go(None, 0, me, ACROSS, True)
    go(z < NZ - 1, 0, me, UP, True)
    go(z > 0, 0, me, DOWN, True)
    go(None, last, me, ACROSS, True)
    for a in range(1, AHEAD):
        send_own(a)
    dots[me * 2 + core] = jnp.zeros((16, states), F32)
    prepare_left()

    for a in range(terms):
        if a + AHEAD < terms:
            send_own(a + AHEAD)
        for h in range(1, NZ):
            ys = [y] if a < last else [y, 1 - y]
            below, above = z >= h, z + h < NZ

            @pl.when(below)
            def _():
                for yy in ys:
                    arrived(a, (z - h) * NY + yy)

            for yy in ys:
                go(below & (z < NZ - 1), a, (z - h) * NY + yy, UP)
            if a < last:
                go(below, a, (z - h) * NY + y, ACROSS)
            for w in slots[(a, 2 * h - 2)]:
                w()

            @pl.when(above)
            def _():
                for yy in ys:
                    arrived(a, (z + h) * NY + yy)

            for yy in ys:
                go(above & (z > 0), a, (z + h) * NY + yy, DOWN)
            if a < last:
                go(above, a, (z + h) * NY + y, ACROSS)
            for w in slots[(a, 2 * h - 1)]:
                w()

    for w in right_work(last - 1):
        w()
    own_copies[last].wait()
    for q in range(6):
        right_piece(last, q * eighth, eighth)
        exchange_piece(q, q * eighth, eighth)

    mine = me * 2 + core
    dot_copies = []
    for k, (pb, pt) in enumerate(peers):
        c = pltpu.make_async_remote_copy(
            src_ref=dots.at[mine], dst_ref=dots.at[mine],
            send_sem=dsend.at[k], recv_sem=drecv.at[mine],
            device_id={"bond": pb, "term": pt}, device_id_type=MESH)
        c.start()
        dot_copies.append(c)
    for k, (pb, pt) in enumerate(peers):
        theirs = pb * 2 + pt
        pltpu.make_async_remote_copy(
            src_ref=dots.at[theirs], dst_ref=dots.at[theirs],
            send_sem=dsend.at[k], recv_sem=drecv.at[theirs],
            device_id={"bond": pb, "term": pt}, device_id_type=MESH).wait_recv()
    total = dots[0]
    for i in range(1, 2 * bond_count):
        total = total + dots[i]
    dot = jnp.sum(total[0:8], axis=(0, 1), keepdims=True)
    norm = jnp.sum(total[8:16], axis=(0, 1), keepdims=True) * 0.5
    theta_ref[...] = jnp.broadcast_to(dot / norm, theta_ref.shape)

    for cond, a, src, way, own in sent:
        def finish(a=a, src=src, way=way, own=own):
            chunk(a, src, way, own).wait_send()

        if cond is None:
            finish()
        else:
            pl.when(cond)(finish)
    for c, d in exchange:
        c.wait()
        d.wait()
    for c in dot_copies:
        c.wait_send()


def fast_body(psi_blocks, left_env, right_env, owner_route, local_sector):
    blocks, states, _ = psi_blocks.shape
    terms, sectors = left_env.shape[0], left_env.shape[1]
    phys = blocks // sectors
    bond_count = NZ * NY
    right_sector = owner_route[:, 0] * sectors + local_sector
    any_spec = pl.BlockSpec(memory_space=pl.ANY)
    block_shape = jax.ShapeDtypeStruct((blocks, states, states), F32)
    dma = pltpu.SemaphoreType.DMA
    part, other, theta = pl.pallas_call(
        functools.partial(kernel, terms, sectors, phys),
        out_shape=(block_shape, block_shape, jax.ShapeDtypeStruct((8, 128), F32)),
        in_specs=[pl.BlockSpec(memory_space=pltpu.SMEM), any_spec, any_spec, any_spec],
        out_specs=(any_spec, any_spec, pl.BlockSpec(memory_space=pltpu.VMEM)),
        scratch_shapes=[pltpu.VMEM((bond_count * sectors, states, states), F32) for _ in range(terms)] + [
            pltpu.VMEM((blocks, states, states), F32),
            pltpu.VMEM((terms, sectors, states, states), F32),
            pltpu.VMEM((sectors, terms * states, 2 * states), BF16),
            pltpu.VMEM((terms, blocks, states, 2 * states), BF16),
            pltpu.VMEM((blocks, states, states), F32),
            pltpu.VMEM((2 * bond_count, 16, states), F32),
            dma((terms, bond_count)),
            dma((terms, bond_count, 3)),
            dma((sectors,)),
            dma,
            dma((terms,)),
            dma((6,)),
            dma((6,)),
            dma((6,)),
            dma((2 * bond_count - 1,)),
            dma((2 * bond_count,)),
        ],
        compiler_params=pltpu.CompilerParams(
            collective_id=0, has_side_effects=True, vmem_limit_bytes=56 * 1024 * 1024),
        cost_estimate=pl.CostEstimate(
            flops=4 * terms * blocks * states ** 3, bytes_accessed=20_000_000, transcendentals=0),
    )(right_sector, psi_blocks, left_env, right_env)
    value = theta[0, 0]
    residual = part + other - value * psi_blocks
    return residual, jnp.reshape(value, (1,))


def general_body(psi_blocks, left_env, right_env, owner_route, local_sector):
    blocks, states, _ = psi_blocks.shape
    sectors = left_env.shape[1]
    phys = blocks // sectors
    right_sector = owner_route[:, 0] * sectors + local_sector
    rights = lax.all_gather(right_env, "bond", axis=1, tiled=True)
    lefts = jnp.arange(blocks, dtype=jnp.int32) // phys

    def one(items):
        block, li, ri = items
        inner = jnp.einsum("aij,jk->aik", jnp.take(left_env, li, axis=1), block, precision=lax.Precision.HIGHEST)
        return jnp.einsum("aik,akl->il", inner, jnp.take(rights, ri, axis=1), precision=lax.Precision.HIGHEST)

    hpsi = lax.psum(lax.map(one, (psi_blocks, lefts, right_sector)), "term")
    sums = lax.psum((jnp.sum(psi_blocks * hpsi), jnp.sum(psi_blocks * psi_blocks)), "bond")
    theta = sums[0] / sums[1]
    return hpsi - theta * psi_blocks, jnp.reshape(theta, (1,))


def solution(mesh):
    fits = mesh.shape["bond"] == NZ * NY and mesh.shape["term"] == 2
    return jax.shard_map(
        fast_body if fits else general_body,
        mesh=mesh,
        in_specs=(
            P(("groups", "bond"), None, None),
            P("term", ("groups", "bond"), None, None),
            P("term", ("groups", "bond"), None, None),
            P(("groups", "bond"), None),
            P(("groups", "bond")),
        ),
        out_specs=(P(("groups", "bond"), None, None), P("groups")),
        check_vma=False,
    )
```

```python
import functools

import jax
import jax.numpy as jnp
from jax import lax
from jax.experimental import pallas as pl
from jax.experimental.pallas import tpu as pltpu
from jax.sharding import PartitionSpec as P

MESH = pl.DeviceIdType.MESH
UP, DOWN, ACROSS = 0, 1, 2
NZ, NY = 4, 2
AHEAD = 2
F32, BF16 = jnp.float32, jnp.bfloat16


def split(x):
    hi = x.astype(BF16)
    lo = (x - hi.astype(F32)).astype(BF16)
    return hi, lo


def pair_rhs(x):
    row = wide(x)
    return jnp.concatenate([row, row], axis=0)


def wide(x):
    hi, lo = split(x)
    return jnp.concatenate([hi, lo], axis=1)


def fold(o):
    n = o.shape[1] // 2
    return o[:, :n] + o[:, n:]


def rows_sum(x):
    r, c = x.shape
    return jnp.sum(x.reshape(r // 8, 8, c), axis=0)


def kernel(terms, sectors, phys, owner_ref, local_ref, psi_hbm, left_hbm, right_hbm,
           out_hbm, theta_ref, *scratch):
    gathered = scratch[:terms]
    (psi_v, left_v, lefts, prods, acc, other, dots,
     recv, send, psi_sem, left_sem, own_sem, xsend, xrecv, out_sem, dsend, drecv) = scratch[terms:]
    bond_count = NZ * NY
    blocks = sectors * phys
    states = psi_v.shape[1]
    me = lax.axis_index("bond")
    core = lax.axis_index("term")
    z, y = me // NY, me % NY
    last = terms - 1

    def rows(src):
        return pl.ds(src * sectors, sectors)

    left_copy = pltpu.make_async_copy(left_hbm, left_v, left_sem)
    left_copy.start()
    psi_copies = []
    for s in range(sectors):
        c = pltpu.make_async_copy(psi_hbm.at[pl.ds(s * phys, phys)], psi_v.at[pl.ds(s * phys, phys)], psi_sem.at[s])
        c.start()
        psi_copies.append(c)
    own_copies = []
    for a in range(terms):
        c = pltpu.make_async_copy(right_hbm.at[a], gathered[a].at[rows(me)], own_sem.at[a])
        c.start()
        own_copies.append(c)

    barrier = pltpu.get_barrier_semaphore()
    peers = []
    for k in range(1, 2 * bond_count):
        flat = lax.rem(me * 2 + core + k, 2 * bond_count)
        peers.append((flat // 2, flat % 2))
    for pb, pt in peers:
        pl.semaphore_signal(barrier, inc=1, device_id={"bond": pb, "term": pt}, device_id_type=MESH)
    pl.semaphore_wait(barrier, len(peers))

    def chunk(a, src, way, own=False):
        if way == UP:
            to = me + NY
        elif way == DOWN:
            to = me - NY
        else:
            to = z * NY + (1 - y)
        here = right_hbm.at[a] if own else gathered[a].at[rows(src)]
        return pltpu.make_async_remote_copy(
            src_ref=here, dst_ref=gathered[a].at[rows(src)],
            send_sem=send.at[a, src, way], recv_sem=recv.at[a, src],
            device_id={"bond": to}, device_id_type=MESH)

    sent = []

    def go(cond, a, src, way, own=False):
        def start():
            chunk(a, src, way, own).start()

        if cond is None:
            start()
        else:
            pl.when(cond)(start)
        sent.append((cond, a, src, way, own))

    def arrived(a, src):
        chunk(a, src, ACROSS).wait_recv()

    partner = z * NY + (1 - y)

    def send_own(a):
        if a < last:
            go(z < NZ - 1, a, me, UP, True)
            go(z > 0, a, me, DOWN, True)
            go(None, a, me, ACROSS, True)
        else:
            go(z < NZ - 1, a, me, UP, True)
            go(z > 0, a, me, DOWN, True)
            arrived(a, partner)
            go(z < NZ - 1, a, partner, UP)
            go(z > 0, a, partner, DOWN)

    def prepare_left():
        left_copy.wait()
        for s in range(sectors):
            for a in range(terms):
                hi, lo = split(left_v[a, s])
                lefts[s, a * states:(a + 1) * states, :] = jnp.concatenate([hi, lo], axis=1)

    def left_piece(s, lo, count):
        def body(i, norm):
            found = []
            for u in range(2):
                b = s * phys + lo + 2 * i + u
                x = psi_v[b]
                t = fold(jnp.dot(lefts[s], pair_rhs(x), preferred_element_type=F32))
                found.append((b, split(t)))
                norm = norm + rows_sum(x * x)
            for b, (hi, low) in found:
                for a in range(terms):
                    cols = slice(a % 2 * states, (a % 2 + 1) * states)
                    prods[a // 2, b, 0:states, cols] = hi[a * states:(a + 1) * states]
                    prods[a // 2, b, states:2 * states, cols] = low[a * states:(a + 1) * states]
            return norm

        norm = lax.fori_loop(0, count // 2, body, jnp.zeros((8, states), F32))
        dots[me * 2 + core, 8:16, :] += norm

    def right_piece(p, first, count):
        final = 2 * p + 1 == last

        def body(i, dot):
            found = []
            for u in range(4):
                b = first + 4 * i + u
                r = owner_ref[b, 0] * sectors + local_ref[b]
                w = jnp.concatenate([wide(gathered[2 * p][r]), wide(gathered[2 * p + 1][r])], axis=0)
                o = fold(jnp.dot(prods[p, b], w, preferred_element_type=F32))
                v = o[:states] + o[states:]
                if p > 0:
                    v = v + acc[b]
                if final:
                    dot = dot + rows_sum(v * psi_v[b])
                found.append((b, v))
            for b, v in found:
                acc[b] = v
            return dot

        dot = lax.fori_loop(0, count // 4, body, jnp.zeros((8, states), F32))
        if final:
            dots[me * 2 + core, 0:8, :] += dot

    def across_done(a):
        own_copies[a].wait()
        for zz in range(NZ):
            arrived(a, zz * NY + (1 - y))

    exchange = []

    def exchange_piece(k, first, count):
        c = pltpu.make_async_remote_copy(
            src_ref=acc.at[pl.ds(first, count)], dst_ref=other.at[pl.ds(first, count)],
            send_sem=xsend.at[k], recv_sem=xrecv.at[k],
            device_id={"term": 1 - core}, device_id_type=MESH)
        c.start()
        exchange.append(c)

    half = phys // 4
    left_work = []
    for s in range(sectors):
        for q in range(4):
            def piece(s=s, q=q):
                if q == 0:
                    psi_copies[s].wait()
                left_piece(s, q * half, half)
            left_work.append(piece)
    eighth = blocks // 6
    twelve = blocks // 4

    slots = {(a, k): [] for a in range(terms) for k in range(6)}
    for i, w in enumerate(left_work):
        slots[(i // 6, i % 6)].append(w)
    for q in range(4):
        def first_pair(q=q):
            if q == 0:
                across_done(0)
                across_done(1)
            right_piece(0, q * twelve, twelve)

        def second_pair(q=q):
            if q == 0:
                across_done(2)
                across_done(3)
            right_piece(1, q * twelve, twelve)

        slots[(3, q)].append(first_pair)
        slots[(5, 2 + q)].append(second_pair)

    go(None, 0, me, ACROSS, True)
    go(z < NZ - 1, 0, me, UP, True)
    go(z > 0, 0, me, DOWN, True)
    go(None, last, me, ACROSS, True)
    for a in range(1, AHEAD):
        send_own(a)
    dots[me * 2 + core] = jnp.zeros((16, states), F32)
    prepare_left()

    for a in range(terms):
        if a + AHEAD < terms:
            send_own(a + AHEAD)
        for h in range(1, NZ):
            ys = [y] if a < last else [y, 1 - y]
            below, above = z >= h, z + h < NZ

            @pl.when(below)
            def _():
                for yy in ys:
                    arrived(a, (z - h) * NY + yy)

            for yy in ys:
                go(below & (z < NZ - 1), a, (z - h) * NY + yy, UP)
            if a < last:
                go(below, a, (z - h) * NY + y, ACROSS)
            for w in slots[(a, 2 * h - 2)]:
                w()

            @pl.when(above)
            def _():
                for yy in ys:
                    arrived(a, (z + h) * NY + yy)

            for yy in ys:
                go(above & (z > 0), a, (z + h) * NY + yy, DOWN)
            if a < last:
                go(above, a, (z + h) * NY + y, ACROSS)
            for w in slots[(a, 2 * h - 1)]:
                w()

    across_done(last - 1)
    own_copies[last].wait()
    for q in range(6):
        right_piece(last // 2, q * eighth, eighth)
        exchange_piece(q, q * eighth, eighth)

    mine = me * 2 + core
    dot_copies = []
    for k, (pb, pt) in enumerate(peers):
        c = pltpu.make_async_remote_copy(
            src_ref=dots.at[mine], dst_ref=dots.at[mine],
            send_sem=dsend.at[k], recv_sem=drecv.at[mine],
            device_id={"bond": pb, "term": pt}, device_id_type=MESH)
        c.start()
        dot_copies.append(c)
    for k, (pb, pt) in enumerate(peers):
        theirs = pb * 2 + pt
        pltpu.make_async_remote_copy(
            src_ref=dots.at[theirs], dst_ref=dots.at[theirs],
            send_sem=dsend.at[k], recv_sem=drecv.at[theirs],
            device_id={"bond": pb, "term": pt}, device_id_type=MESH).wait_recv()
    total = dots[0]
    for i in range(1, 2 * bond_count):
        total = total + dots[i]
    dot = jnp.sum(total[0:8], axis=(0, 1), keepdims=True)
    norm = jnp.sum(total[8:16], axis=(0, 1), keepdims=True) * 0.5
    theta = dot / norm
    theta_ref[0] = theta[0, 0]
    outs = []
    for q in range(6):
        exchange[q].wait()

        def finish_block(i, carry, q=q):
            b = q * eighth + i
            acc[b] = acc[b] + other[b] - theta * psi_v[b]
            return carry

        lax.fori_loop(0, eighth, finish_block, 0)
        d = pltpu.make_async_copy(acc.at[pl.ds(q * eighth, eighth)], out_hbm.at[pl.ds(q * eighth, eighth)], out_sem.at[q])
        d.start()
        outs.append(d)

    for cond, a, src, way, own in sent:
        def finish(a=a, src=src, way=way, own=own):
            chunk(a, src, way, own).wait_send()

        if cond is None:
            finish()
        else:
            pl.when(cond)(finish)
    for d in outs:
        d.wait()
    for c in dot_copies:
        c.wait_send()


def fast_body(psi_blocks, left_env, right_env, owner_route, local_sector):
    blocks, states, _ = psi_blocks.shape
    terms, sectors = left_env.shape[0], left_env.shape[1]
    phys = blocks // sectors
    bond_count = NZ * NY
    any_spec = pl.BlockSpec(memory_space=pl.ANY)
    block_shape = jax.ShapeDtypeStruct((blocks, states, states), F32)
    dma = pltpu.SemaphoreType.DMA
    return pl.pallas_call(
        functools.partial(kernel, terms, sectors, phys),
        out_shape=(block_shape, jax.ShapeDtypeStruct((1,), F32)),
        in_specs=[pl.BlockSpec(memory_space=pltpu.SMEM), pl.BlockSpec(memory_space=pltpu.SMEM), any_spec, any_spec, any_spec],
        out_specs=(any_spec, pl.BlockSpec(memory_space=pltpu.SMEM)),
        scratch_shapes=[pltpu.VMEM((bond_count * sectors, states, states), F32) for _ in range(terms)] + [
            pltpu.VMEM((blocks, states, states), F32),
            pltpu.VMEM((terms, sectors, states, states), F32),
            pltpu.VMEM((sectors, terms * states, 2 * states), BF16),
            pltpu.VMEM((terms // 2, blocks, 2 * states, 2 * states), BF16),
            pltpu.VMEM((blocks, states, states), F32),
            pltpu.VMEM((blocks, states, states), F32),
            pltpu.VMEM((2 * bond_count, 16, states), F32),
            dma((terms, bond_count)),
            dma((terms, bond_count, 3)),
            dma((sectors,)),
            dma,
            dma((terms,)),
            dma((6,)),
            dma((6,)),
            dma((6,)),
            dma((2 * bond_count - 1,)),
            dma((2 * bond_count,)),
        ],
        compiler_params=pltpu.CompilerParams(
            collective_id=0, has_side_effects=True, vmem_limit_bytes=56 * 1024 * 1024),
        cost_estimate=pl.CostEstimate(
            flops=4 * terms * blocks * states ** 3, bytes_accessed=20_000_000, transcendentals=0),
    )(owner_route, local_sector, psi_blocks, left_env, right_env)


def general_body(psi_blocks, left_env, right_env, owner_route, local_sector):
    blocks, states, _ = psi_blocks.shape
    sectors = left_env.shape[1]
    phys = blocks // sectors
    right_sector = owner_route[:, 0] * sectors + local_sector
    rights = lax.all_gather(right_env, "bond", axis=1, tiled=True)
    lefts = jnp.arange(blocks, dtype=jnp.int32) // phys

    def one(items):
        block, li, ri = items
        inner = jnp.einsum("aij,jk->aik", jnp.take(left_env, li, axis=1), block, precision=lax.Precision.HIGHEST)
        return jnp.einsum("aik,akl->il", inner, jnp.take(rights, ri, axis=1), precision=lax.Precision.HIGHEST)

    hpsi = lax.psum(lax.map(one, (psi_blocks, lefts, right_sector)), "term")
    sums = lax.psum((jnp.sum(psi_blocks * hpsi), jnp.sum(psi_blocks * psi_blocks)), "bond")
    theta = sums[0] / sums[1]
    return hpsi - theta * psi_blocks, jnp.reshape(theta, (1,))


def solution(mesh):
    fits = mesh.shape["bond"] == NZ * NY and mesh.shape["term"] == 2
    return jax.shard_map(
        fast_body if fits else general_body,
        mesh=mesh,
        in_specs=(
            P(("groups", "bond"), None, None),
            P("term", ("groups", "bond"), None, None),
            P("term", ("groups", "bond"), None, None),
            P(("groups", "bond"), None),
            P(("groups", "bond")),
        ),
        out_specs=(P(("groups", "bond"), None, None), P("groups")),
        check_vma=False,
    )
```

```python
import functools

import jax
import jax.numpy as jnp
from jax import lax
from jax.experimental import pallas as pl
from jax.experimental.pallas import tpu as pltpu
from jax.sharding import PartitionSpec as P

MESH = pl.DeviceIdType.MESH
UP, DOWN, ACROSS = 0, 1, 2
NZ, NY = 4, 2
AHEAD = 2
F32, BF16 = jnp.float32, jnp.bfloat16


def split(x):
    hi = x.astype(BF16)
    lo = (x - hi.astype(F32)).astype(BF16)
    return hi, lo


def pair_rhs(x):
    row = wide(x)
    return jnp.concatenate([row, row], axis=0)


def wide(x):
    hi, lo = split(x)
    return jnp.concatenate([hi, lo], axis=1)


def fold(o):
    n = o.shape[1] // 2
    return o[:, :n] + o[:, n:]


def rows_sum(x):
    r, c = x.shape
    return jnp.sum(x.reshape(r // 8, 8, c), axis=0)


def kernel(terms, sectors, phys, owner_ref, local_ref, psi_hbm, left_hbm, right_hbm,
           out_hbm, theta_ref, *scratch):
    gathered = scratch[:terms]
    (psi_v, left_v, lefts, prods, acc, other, dots,
     recv, send, psi_sem, left_sem, own_sem, xsend, xrecv, out_sem, dsend, drecv) = scratch[terms:]
    bond_count = NZ * NY
    blocks = sectors * phys
    states = psi_v.shape[1]
    me = lax.axis_index("bond")
    core = lax.axis_index("term")
    z, y = me // NY, me % NY
    last = terms - 1

    def rows(src):
        return pl.ds(src * sectors, sectors)

    left_copy = pltpu.make_async_copy(left_hbm, left_v, left_sem)
    left_copy.start()
    psi_copies = []
    for s in range(sectors):
        c = pltpu.make_async_copy(psi_hbm.at[pl.ds(s * phys, phys)], psi_v.at[pl.ds(s * phys, phys)], psi_sem.at[s])
        c.start()
        psi_copies.append(c)
    own_copies = []
    for a in range(terms):
        c = pltpu.make_async_copy(right_hbm.at[a], gathered[a].at[rows(me)], own_sem.at[a])
        c.start()
        own_copies.append(c)

    barrier = pltpu.get_barrier_semaphore()
    peers = []
    for k in range(1, 2 * bond_count):
        flat = lax.rem(me * 2 + core + k, 2 * bond_count)
        peers.append((flat // 2, flat % 2))
    for pb, pt in peers:
        pl.semaphore_signal(barrier, inc=1, device_id={"bond": pb, "term": pt}, device_id_type=MESH)
    pl.semaphore_wait(barrier, len(peers))

    def chunk(a, src, way, own=False):
        if way == UP:
            to = me + NY
        elif way == DOWN:
            to = me - NY
        else:
            to = z * NY + (1 - y)
        here = right_hbm.at[a] if own else gathered[a].at[rows(src)]
        return pltpu.make_async_remote_copy(
            src_ref=here, dst_ref=gathered[a].at[rows(src)],
            send_sem=send.at[a, src, way], recv_sem=recv.at[a, src],
            device_id={"bond": to}, device_id_type=MESH)

    sent = []

    def go(cond, a, src, way, own=False):
        def start():
            chunk(a, src, way, own).start()

        if cond is None:
            start()
        else:
            pl.when(cond)(start)
        sent.append((cond, a, src, way, own))

    def arrived(a, src):
        chunk(a, src, ACROSS).wait_recv()

    partner = z * NY + (1 - y)

    def send_own(a):
        if a < last:
            go(z < NZ - 1, a, me, UP, True)
            go(z > 0, a, me, DOWN, True)
            go(None, a, me, ACROSS, True)
        else:
            go(z < NZ - 1, a, me, UP, True)
            go(z > 0, a, me, DOWN, True)
            arrived(a, partner)
            go(z < NZ - 1, a, partner, UP)
            go(z > 0, a, partner, DOWN)

    def prepare_left():
        left_copy.wait()
        for s in range(sectors):
            for a in range(terms):
                hi, lo = split(left_v[a, s])
                lefts[s, a * states:(a + 1) * states, :] = jnp.concatenate([hi, lo], axis=1)

    def left_piece(s, lo, count):
        def body(i, norm):
            found = []
            for u in range(2):
                b = s * phys + lo + 2 * i + u
                x = psi_v[b]
                t = fold(jnp.dot(lefts[s], pair_rhs(x), preferred_element_type=F32))
                found.append((b, split(t)))
                norm = norm + rows_sum(x * x)
            for b, (hi, low) in found:
                for a in range(terms):
                    cols = slice(a % 2 * states, (a % 2 + 1) * states)
                    prods[a // 2, b, 0:states, cols] = hi[a * states:(a + 1) * states]
                    prods[a // 2, b, states:2 * states, cols] = low[a * states:(a + 1) * states]
            return norm

        norm = lax.fori_loop(0, count // 2, body, jnp.zeros((8, states), F32))
        dots[me * 2 + core, 8:16, :] += norm

    def right_piece(p, first, count):
        final = 2 * p + 1 == last

        def body(i, dot):
            found = []
            for u in range(4):
                b = first + 4 * i + u
                r = owner_ref[b] * sectors + local_ref[b]
                w = jnp.concatenate([wide(gathered[2 * p][r]), wide(gathered[2 * p + 1][r])], axis=0)
                o = fold(jnp.dot(prods[p, b], w, preferred_element_type=F32))
                v = o[:states] + o[states:]
                if p > 0:
                    v = v + acc[b]
                if final:
                    dot = dot + rows_sum(v * psi_v[b])
                found.append((b, v))
            for b, v in found:
                acc[b] = v
            return dot

        dot = lax.fori_loop(0, count // 4, body, jnp.zeros((8, states), F32))
        if final:
            dots[me * 2 + core, 0:8, :] += dot

    def across_done(a):
        own_copies[a].wait()
        for zz in range(NZ):
            arrived(a, zz * NY + (1 - y))

    exchange = []

    def exchange_piece(k, first, count):
        c = pltpu.make_async_remote_copy(
            src_ref=acc.at[pl.ds(first, count)], dst_ref=other.at[pl.ds(first, count)],
            send_sem=xsend.at[k], recv_sem=xrecv.at[k],
            device_id={"term": 1 - core}, device_id_type=MESH)
        c.start()
        exchange.append(c)

    half = phys // 4
    left_work = []
    for s in range(sectors):
        for q in range(4):
            def piece(s=s, q=q):
                if q == 0:
                    psi_copies[s].wait()
                left_piece(s, q * half, half)
            left_work.append(piece)
    eighth = blocks // 6
    twelve = blocks // 4

    slots = {(a, k): [] for a in range(terms) for k in range(6)}
    for i, w in enumerate(left_work):
        slots[(i // 6, i % 6)].append(w)
    for q in range(4):
        def first_pair(q=q):
            if q == 0:
                across_done(0)
                across_done(1)
            right_piece(0, q * twelve, twelve)

        def second_pair(q=q):
            if q == 0:
                across_done(2)
                across_done(3)
            right_piece(1, q * twelve, twelve)

        slots[(3, q)].append(first_pair)
        slots[(5, 2 + q)].append(second_pair)

    go(None, 0, me, ACROSS, True)
    go(z < NZ - 1, 0, me, UP, True)
    go(z > 0, 0, me, DOWN, True)
    go(None, last, me, ACROSS, True)
    for a in range(1, AHEAD):
        send_own(a)
    dots[me * 2 + core] = jnp.zeros((16, states), F32)
    prepare_left()

    for a in range(terms):
        if a + AHEAD < terms:
            send_own(a + AHEAD)
        for h in range(1, NZ):
            ys = [y] if a < last else [y, 1 - y]
            below, above = z >= h, z + h < NZ

            @pl.when(below)
            def _():
                for yy in ys:
                    arrived(a, (z - h) * NY + yy)

            for yy in ys:
                go(below & (z < NZ - 1), a, (z - h) * NY + yy, UP)
            if a < last:
                go(below, a, (z - h) * NY + y, ACROSS)
            for w in slots[(a, 2 * h - 2)]:
                w()

            @pl.when(above)
            def _():
                for yy in ys:
                    arrived(a, (z + h) * NY + yy)

            for yy in ys:
                go(above & (z > 0), a, (z + h) * NY + yy, DOWN)
            if a < last:
                go(above, a, (z + h) * NY + y, ACROSS)
            for w in slots[(a, 2 * h - 1)]:
                w()

    across_done(last - 1)
    own_copies[last].wait()
    for q in range(6):
        right_piece(last // 2, q * eighth, eighth)
        exchange_piece(q, q * eighth, eighth)

    mine = me * 2 + core
    dot_copies = []
    for k, (pb, pt) in enumerate(peers):
        c = pltpu.make_async_remote_copy(
            src_ref=dots.at[mine], dst_ref=dots.at[mine],
            send_sem=dsend.at[k], recv_sem=drecv.at[mine],
            device_id={"bond": pb, "term": pt}, device_id_type=MESH)
        c.start()
        dot_copies.append(c)
    outs = []
    for q in range(6):
        exchange[q].wait()

        def finish_block(i, carry, q=q):
            b = q * eighth + i
            acc[b] = acc[b] + other[b]
            return carry

        lax.fori_loop(0, eighth, finish_block, 0)
        d = pltpu.make_async_copy(acc.at[pl.ds(q * eighth, eighth)], out_hbm.at[pl.ds(q * eighth, eighth)], out_sem.at[q])
        d.start()
        outs.append(d)
    for k, (pb, pt) in enumerate(peers):
        theirs = pb * 2 + pt
        pltpu.make_async_remote_copy(
            src_ref=dots.at[theirs], dst_ref=dots.at[theirs],
            send_sem=dsend.at[k], recv_sem=drecv.at[theirs],
            device_id={"bond": pb, "term": pt}, device_id_type=MESH).wait_recv()
    total = dots[0]
    for i in range(1, 2 * bond_count):
        total = total + dots[i]
    dot = jnp.sum(total[0:8], axis=(0, 1), keepdims=True)
    norm = jnp.sum(total[8:16], axis=(0, 1), keepdims=True) * 0.5
    theta = dot / norm
    theta_ref[0] = theta[0, 0]
    for cond, a, src, way, own in sent:
        def finish(a=a, src=src, way=way, own=own):
            chunk(a, src, way, own).wait_send()

        if cond is None:
            finish()
        else:
            pl.when(cond)(finish)
    for d in outs:
        d.wait()
    for c in dot_copies:
        c.wait_send()


def fast_body(psi_blocks, left_env, right_env, owner_route, local_sector):
    blocks, states, _ = psi_blocks.shape
    terms, sectors = left_env.shape[0], left_env.shape[1]
    phys = blocks // sectors
    bond_count = NZ * NY
    any_spec = pl.BlockSpec(memory_space=pl.ANY)
    block_shape = jax.ShapeDtypeStruct((blocks, states, states), F32)
    dma = pltpu.SemaphoreType.DMA
    hpsi, theta = pl.pallas_call(
        functools.partial(kernel, terms, sectors, phys),
        out_shape=(block_shape, jax.ShapeDtypeStruct((1,), F32)),
        in_specs=[pl.BlockSpec(memory_space=pltpu.SMEM), pl.BlockSpec(memory_space=pltpu.SMEM), any_spec, any_spec, any_spec],
        out_specs=(any_spec, pl.BlockSpec(memory_space=pltpu.SMEM)),
        scratch_shapes=[pltpu.VMEM((bond_count * sectors, states, states), F32) for _ in range(terms)] + [
            pltpu.VMEM((blocks, states, states), F32),
            pltpu.VMEM((terms, sectors, states, states), F32),
            pltpu.VMEM((sectors, terms * states, 2 * states), BF16),
            pltpu.VMEM((terms // 2, blocks, 2 * states, 2 * states), BF16),
            pltpu.VMEM((blocks, states, states), F32),
            pltpu.VMEM((blocks, states, states), F32),
            pltpu.VMEM((2 * bond_count, 16, states), F32),
            dma((terms, bond_count)),
            dma((terms, bond_count, 3)),
            dma((sectors,)),
            dma,
            dma((terms,)),
            dma((6,)),
            dma((6,)),
            dma((6,)),
            dma((2 * bond_count - 1,)),
            dma((2 * bond_count,)),
        ],
        compiler_params=pltpu.CompilerParams(
            collective_id=0, has_side_effects=True, vmem_limit_bytes=56 * 1024 * 1024),
        cost_estimate=pl.CostEstimate(
            flops=4 * terms * blocks * states ** 3, bytes_accessed=20_000_000, transcendentals=0),
    )(owner_route.reshape(blocks), local_sector, psi_blocks, left_env, right_env)
    return hpsi - theta[0] * psi_blocks, theta


def general_body(psi_blocks, left_env, right_env, owner_route, local_sector):
    blocks, states, _ = psi_blocks.shape
    sectors = left_env.shape[1]
    phys = blocks // sectors
    right_sector = owner_route[:, 0] * sectors + local_sector
    rights = lax.all_gather(right_env, "bond", axis=1, tiled=True)
    lefts = jnp.arange(blocks, dtype=jnp.int32) // phys

    def one(items):
        block, li, ri = items
        inner = jnp.einsum("aij,jk->aik", jnp.take(left_env, li, axis=1), block, precision=lax.Precision.HIGHEST)
        return jnp.einsum("aik,akl->il", inner, jnp.take(rights, ri, axis=1), precision=lax.Precision.HIGHEST)

    hpsi = lax.psum(lax.map(one, (psi_blocks, lefts, right_sector)), "term")
    sums = lax.psum((jnp.sum(psi_blocks * hpsi), jnp.sum(psi_blocks * psi_blocks)), "bond")
    theta = sums[0] / sums[1]
    return hpsi - theta * psi_blocks, jnp.reshape(theta, (1,))


def solution(mesh):
    fits = mesh.shape["bond"] == NZ * NY and mesh.shape["term"] == 2
    return jax.shard_map(
        fast_body if fits else general_body,
        mesh=mesh,
        in_specs=(
            P(("groups", "bond"), None, None),
            P("term", ("groups", "bond"), None, None),
            P("term", ("groups", "bond"), None, None),
            P(("groups", "bond"), None),
            P(("groups", "bond")),
        ),
        out_specs=(P(("groups", "bond"), None, None), P("groups")),
        check_vma=False,
    )
```

```python
import functools

import jax
import jax.numpy as jnp
from jax import lax
from jax.experimental import pallas as pl
from jax.experimental.pallas import tpu as pltpu
from jax.sharding import PartitionSpec as P

MESH = pl.DeviceIdType.MESH
UP, DOWN, ACROSS = 0, 1, 2
NZ, NY = 4, 2
AHEAD = 2
F32, BF16 = jnp.float32, jnp.bfloat16


def split(x):
    hi = x.astype(BF16)
    lo = (x - hi.astype(F32)).astype(BF16)
    return hi, lo


def pair_rhs(x):
    row = wide(x)
    return jnp.concatenate([row, row], axis=0)


def wide(x):
    hi, lo = split(x)
    return jnp.concatenate([hi, lo], axis=1)


def fold(o):
    n = o.shape[1] // 2
    return o[:, :n] + o[:, n:]


def rows_sum(x):
    r, c = x.shape
    return jnp.sum(x.reshape(r // 8, 8, c), axis=0)


def kernel(terms, sectors, phys, owner_ref, local_ref, psi_hbm, left_hbm, right_hbm,
           out_hbm, theta_ref, *scratch):
    gathered = scratch[:terms]
    (psi_v, left_v, lefts, prods, acc, other, dots,
     recv, send, psi_sem, left_sem, own_sem, xsend, xrecv, out_sem, dsend, drecv) = scratch[terms:]
    bond_count = NZ * NY
    blocks = sectors * phys
    states = psi_v.shape[1]
    me = lax.axis_index("bond")
    core = lax.axis_index("term")
    z, y = me // NY, me % NY
    last = terms - 1

    def rows(src):
        return pl.ds(src * sectors, sectors)

    left_copy = pltpu.make_async_copy(left_hbm, left_v, left_sem)
    left_copy.start()
    psi_copies = []
    for s in range(sectors):
        c = pltpu.make_async_copy(psi_hbm.at[pl.ds(s * phys, phys)], psi_v.at[pl.ds(s * phys, phys)], psi_sem.at[s])
        c.start()
        psi_copies.append(c)
    own_copies = []
    for a in range(terms):
        c = pltpu.make_async_copy(right_hbm.at[a], gathered[a].at[rows(me)], own_sem.at[a])
        c.start()
        own_copies.append(c)

    barrier = pltpu.get_barrier_semaphore()
    peers = []
    for k in range(1, 2 * bond_count):
        flat = lax.rem(me * 2 + core + k, 2 * bond_count)
        peers.append((flat // 2, flat % 2))
    for pb, pt in peers:
        pl.semaphore_signal(barrier, inc=1, device_id={"bond": pb, "term": pt}, device_id_type=MESH)
    pl.semaphore_wait(barrier, len(peers))

    def chunk(a, src, way, own=False):
        if way == UP:
            to = me + NY
        elif way == DOWN:
            to = me - NY
        else:
            to = z * NY + (1 - y)
        here = right_hbm.at[a] if own else gathered[a].at[rows(src)]
        return pltpu.make_async_remote_copy(
            src_ref=here, dst_ref=gathered[a].at[rows(src)],
            send_sem=send.at[a, src, way], recv_sem=recv.at[a, src],
            device_id={"bond": to}, device_id_type=MESH)

    sent = []

    def go(cond, a, src, way, own=False):
        def start():
            chunk(a, src, way, own).start()

        if cond is None:
            start()
        else:
            pl.when(cond)(start)
        sent.append((cond, a, src, way, own))

    def arrived(a, src):
        chunk(a, src, ACROSS).wait_recv()

    partner = z * NY + (1 - y)

    def send_own(a):
        if a < last:
            go(z < NZ - 1, a, me, UP, True)
            go(z > 0, a, me, DOWN, True)
            go(None, a, me, ACROSS, True)
        else:
            go(z < NZ - 1, a, me, UP, True)
            go(z > 0, a, me, DOWN, True)
            arrived(a, partner)
            go(z < NZ - 1, a, partner, UP)
            go(z > 0, a, partner, DOWN)

    def prepare_left():
        left_copy.wait()
        for s in range(sectors):
            for a in range(terms):
                hi, lo = split(left_v[a, s])
                lefts[s, a * states:(a + 1) * states, :] = jnp.concatenate([hi, lo], axis=1)

    def left_piece(s, lo, count):
        def body(i, norm):
            found = []
            for u in range(2):
                b = s * phys + lo + 2 * i + u
                x = psi_v[b]
                t = fold(jnp.dot(lefts[s], pair_rhs(x), preferred_element_type=F32))
                found.append((b, split(t)))
                norm = norm + rows_sum(x * x)
            for b, (hi, low) in found:
                for a in range(terms):
                    cols = slice(a % 2 * states, (a % 2 + 1) * states)
                    prods[a // 2, b, 0:states, cols] = hi[a * states:(a + 1) * states]
                    prods[a // 2, b, states:2 * states, cols] = low[a * states:(a + 1) * states]
            return norm

        norm = lax.fori_loop(0, count // 2, body, jnp.zeros((8, states), F32))
        dots[me * 2 + core, 8:16, :] += norm

    def right_piece(p, first, count):
        final = 2 * p + 1 == last

        def body(i, dot):
            found = []
            for u in range(8):
                b = first + 8 * i + u
                r = owner_ref[b] * sectors + local_ref[b]
                w = jnp.concatenate([wide(gathered[2 * p][r]), wide(gathered[2 * p + 1][r])], axis=0)
                o = fold(jnp.dot(prods[p, b], w, preferred_element_type=F32))
                v = o[:states] + o[states:]
                if p > 0:
                    v = v + acc[b]
                if final:
                    dot = dot + rows_sum(v * psi_v[b])
                found.append((b, v))
            for b, v in found:
                acc[b] = v
            return dot

        dot = lax.fori_loop(0, count // 8, body, jnp.zeros((8, states), F32))
        if final:
            dots[me * 2 + core, 0:8, :] += dot

    def across_done(a):
        own_copies[a].wait()
        for zz in range(NZ):
            arrived(a, zz * NY + (1 - y))

    exchange = []

    def exchange_piece(k, first, count):
        c = pltpu.make_async_remote_copy(
            src_ref=acc.at[pl.ds(first, count)], dst_ref=other.at[pl.ds(first, count)],
            send_sem=xsend.at[k], recv_sem=xrecv.at[k],
            device_id={"term": 1 - core}, device_id_type=MESH)
        c.start()
        exchange.append(c)

    half = phys // 4
    left_work = []
    for s in range(sectors):
        for q in range(4):
            def piece(s=s, q=q):
                if q == 0:
                    psi_copies[s].wait()
                left_piece(s, q * half, half)
            left_work.append(piece)
    eighth = blocks // 6
    third = blocks // 3

    slots = {(a, k): [] for a in range(terms) for k in range(6)}
    for i, w in enumerate(left_work):
        slots[(i // 6, i % 6)].append(w)
    for q in range(3):
        def first_pair(q=q):
            if q == 0:
                across_done(0)
                across_done(1)
            right_piece(0, q * third, third)

        def second_pair(q=q):
            if q == 0:
                across_done(2)
                across_done(3)
            right_piece(1, q * third, third)

        slots[(3, q)].append(first_pair)
        slots[(5, 1 + q)].append(second_pair)

    go(None, 0, me, ACROSS, True)
    go(z < NZ - 1, 0, me, UP, True)
    go(z > 0, 0, me, DOWN, True)
    go(None, last, me, ACROSS, True)
    for a in range(1, AHEAD):
        send_own(a)
    dots[me * 2 + core] = jnp.zeros((16, states), F32)
    prepare_left()

    for a in range(terms):
        if a + AHEAD < terms:
            send_own(a + AHEAD)
        for h in range(1, NZ):
            ys = [y] if a < last else [y, 1 - y]
            below, above = z >= h, z + h < NZ

            @pl.when(below)
            def _():
                for yy in ys:
                    arrived(a, (z - h) * NY + yy)

            for yy in ys:
                go(below & (z < NZ - 1), a, (z - h) * NY + yy, UP)
            if a < last:
                go(below, a, (z - h) * NY + y, ACROSS)
            for w in slots[(a, 2 * h - 2)]:
                w()

            @pl.when(above)
            def _():
                for yy in ys:
                    arrived(a, (z + h) * NY + yy)

            for yy in ys:
                go(above & (z > 0), a, (z + h) * NY + yy, DOWN)
            if a < last:
                go(above, a, (z + h) * NY + y, ACROSS)
            for w in slots[(a, 2 * h - 1)]:
                w()

    across_done(last - 1)
    own_copies[last].wait()
    for q in range(6):
        right_piece(last // 2, q * eighth, eighth)
        exchange_piece(q, q * eighth, eighth)

    mine = me * 2 + core
    dot_copies = []
    for k, (pb, pt) in enumerate(peers):
        c = pltpu.make_async_remote_copy(
            src_ref=dots.at[mine], dst_ref=dots.at[mine],
            send_sem=dsend.at[k], recv_sem=drecv.at[mine],
            device_id={"bond": pb, "term": pt}, device_id_type=MESH)
        c.start()
        dot_copies.append(c)
    outs = []
    for q in range(6):
        exchange[q].wait()

        def finish_block(i, carry, q=q):
            b = q * eighth + i
            acc[b] = acc[b] + other[b]
            return carry

        lax.fori_loop(0, eighth, finish_block, 0)
        d = pltpu.make_async_copy(acc.at[pl.ds(q * eighth, eighth)], out_hbm.at[pl.ds(q * eighth, eighth)], out_sem.at[q])
        d.start()
        outs.append(d)
    for k, (pb, pt) in enumerate(peers):
        theirs = pb * 2 + pt
        pltpu.make_async_remote_copy(
            src_ref=dots.at[theirs], dst_ref=dots.at[theirs],
            send_sem=dsend.at[k], recv_sem=drecv.at[theirs],
            device_id={"bond": pb, "term": pt}, device_id_type=MESH).wait_recv()
    total = dots[0]
    for i in range(1, 2 * bond_count):
        total = total + dots[i]
    dot = jnp.sum(total[0:8], axis=(0, 1), keepdims=True)
    norm = jnp.sum(total[8:16], axis=(0, 1), keepdims=True) * 0.5
    theta = dot / norm
    theta_ref[0] = theta[0, 0]
    for cond, a, src, way, own in sent:
        def finish(a=a, src=src, way=way, own=own):
            chunk(a, src, way, own).wait_send()

        if cond is None:
            finish()
        else:
            pl.when(cond)(finish)
    for d in outs:
        d.wait()
    for c in dot_copies:
        c.wait_send()


def fast_body(psi_blocks, left_env, right_env, owner_route, local_sector):
    blocks, states, _ = psi_blocks.shape
    terms, sectors = left_env.shape[0], left_env.shape[1]
    phys = blocks // sectors
    bond_count = NZ * NY
    any_spec = pl.BlockSpec(memory_space=pl.ANY)
    block_shape = jax.ShapeDtypeStruct((blocks, states, states), F32)
    dma = pltpu.SemaphoreType.DMA
    hpsi, theta = pl.pallas_call(
        functools.partial(kernel, terms, sectors, phys),
        out_shape=(block_shape, jax.ShapeDtypeStruct((1,), F32)),
        in_specs=[pl.BlockSpec(memory_space=pltpu.SMEM), pl.BlockSpec(memory_space=pltpu.SMEM), any_spec, any_spec, any_spec],
        out_specs=(any_spec, pl.BlockSpec(memory_space=pltpu.SMEM)),
        scratch_shapes=[pltpu.VMEM((bond_count * sectors, states, states), F32) for _ in range(terms)] + [
            pltpu.VMEM((blocks, states, states), F32),
            pltpu.VMEM((terms, sectors, states, states), F32),
            pltpu.VMEM((sectors, terms * states, 2 * states), BF16),
            pltpu.VMEM((terms // 2, blocks, 2 * states, 2 * states), BF16),
            pltpu.VMEM((blocks, states, states), F32),
            pltpu.VMEM((blocks, states, states), F32),
            pltpu.VMEM((2 * bond_count, 16, states), F32),
            dma((terms, bond_count)),
            dma((terms, bond_count, 3)),
            dma((sectors,)),
            dma,
            dma((terms,)),
            dma((6,)),
            dma((6,)),
            dma((6,)),
            dma((2 * bond_count - 1,)),
            dma((2 * bond_count,)),
        ],
        compiler_params=pltpu.CompilerParams(
            collective_id=0, has_side_effects=True, vmem_limit_bytes=56 * 1024 * 1024),
        cost_estimate=pl.CostEstimate(
            flops=4 * terms * blocks * states ** 3, bytes_accessed=20_000_000, transcendentals=0),
    )(owner_route.reshape(blocks), local_sector, psi_blocks, left_env, right_env)
    return hpsi - theta[0] * psi_blocks, theta


def general_body(psi_blocks, left_env, right_env, owner_route, local_sector):
    blocks, states, _ = psi_blocks.shape
    sectors = left_env.shape[1]
    phys = blocks // sectors
    right_sector = owner_route[:, 0] * sectors + local_sector
    rights = lax.all_gather(right_env, "bond", axis=1, tiled=True)
    lefts = jnp.arange(blocks, dtype=jnp.int32) // phys

    def one(items):
        block, li, ri = items
        inner = jnp.einsum("aij,jk->aik", jnp.take(left_env, li, axis=1), block, precision=lax.Precision.HIGHEST)
        return jnp.einsum("aik,akl->il", inner, jnp.take(rights, ri, axis=1), precision=lax.Precision.HIGHEST)

    hpsi = lax.psum(lax.map(one, (psi_blocks, lefts, right_sector)), "term")
    sums = lax.psum((jnp.sum(psi_blocks * hpsi), jnp.sum(psi_blocks * psi_blocks)), "bond")
    theta = sums[0] / sums[1]
    return hpsi - theta * psi_blocks, jnp.reshape(theta, (1,))


def solution(mesh):
    fits = mesh.shape["bond"] == NZ * NY and mesh.shape["term"] == 2
    return jax.shard_map(
        fast_body if fits else general_body,
        mesh=mesh,
        in_specs=(
            P(("groups", "bond"), None, None),
            P("term", ("groups", "bond"), None, None),
            P("term", ("groups", "bond"), None, None),
            P(("groups", "bond"), None),
            P(("groups", "bond")),
        ),
        out_specs=(P(("groups", "bond"), None, None), P("groups")),
        check_vma=False,
    )
```
